512 devices in a mesh: pair: 64 (over x, z), ri: 8 (over y, core).
Axes of the slice: x: 4, y: 4, z: 16, core: 2. Of those that a mesh axis runs over, the one named last changes fastest.
Arguments:
- tensor: bfloat16 [64, 2048, 2304], P('pair', 'ri'), may hold values from -0.5 to 0.5
- pattern: int32 [64, 64], P('pair', 'ri'), may hold values 0 or 1
- pair_blocks: int32 [64, 2], replicated, may hold values from 0 to 11, as said below
- green_occ: bfloat16 [576, 576], replicated, may hold values from -0.25 to 0.25
- green_virt: bfloat16 [576, 576], replicated, may hold values from -0.25 to 0.25
Outputs:
- chi: float32 [2048, 2048], P('ri', 'pair')
The draws below stay inside these ranges and needn't reach their ends.
Inputs may be any that keep to these rules, and one draw needn't show every extreme that they name: `pair_blocks`: no pair of blocks appears twice.
All inputs are finite; a program needn't handle non-finite values. No bound on the sum of `pattern` on one device may be relied on, other than what follows from the above.
Results may differ from the reference program's by a relative error of at most 0.0041.
Values may be sent and summed in bfloat16 or wider, within the bound.
A program may use at most 64 MiB of HBM per device.

```python
import jax
import jax.numpy as jnp
from jax import lax

BLK = 48
NB = 12
RI_W = 2048
RB = 32
NBF = 576
BB = 2304
NPAIRS = 64
NRB = 64


def draw_pair_blocks(key, part):
    key = jax.random.fold_in(key, 7)
    chosen = jax.random.permutation(key, NB * NB)[:NPAIRS]
    return jnp.stack([chosen // NB, chosen % NB], axis=1).astype(jnp.int32)


def with_ends(values, own_key, smallest, top_value):
    shape = values.shape
    place = [jax.random.randint(jax.random.fold_in(own_key, axis), (), 0, shape[axis]) for axis in range(len(shape))]
    values = values.at[tuple(place)].set(smallest)
    longest = shape.index(max(shape))
    place[longest] = (place[longest] + 1) % shape[longest]
    return values.at[tuple(place)].set(top_value)


def steps_of(own_key, extent, split, least, high):
    gain = 1.0
    for position, blocks in split:
        draws = jax.random.uniform(jax.random.fold_in(jax.random.fold_in(own_key, 6), position), (blocks,), jnp.float32, least / len(split), high / len(split))
        gain = gain * jnp.repeat(jnp.exp(draws), extent[position] // blocks).reshape((-1,) + (1,) * (len(extent) - 1 - position))
    return gain


def normal_values(key, dims, spread, bound, cuts=(), kind=jnp.bfloat16):
    entries = spread * jax.random.normal(key, dims, jnp.float32)
    if cuts:
        entries = entries * steps_of(key, dims, cuts, -0.22, 0.18)
    return jnp.clip(entries, -bound, bound).astype(kind)


def setup_inputs(seed: int = 0) -> dict:
    arg_keys = jax.random.split(jax.random.key(seed), 6)
    return {
        "tensor": normal_values(arg_keys[0], (NPAIRS, RI_W, BB), 0.08, 0.5, ((0, 64), (1, 8))),
        "pattern": with_ends((jax.random.randint(arg_keys[1], (NPAIRS, NRB), 0, 4) < 3).astype(jnp.int32), jax.random.fold_in(arg_keys[1], 1), 0, 1),
        "pair_blocks": draw_pair_blocks(jax.random.fold_in(arg_keys[5], 71), 0),
        "green_occ": normal_values(arg_keys[3], (NBF, NBF), NBF ** -0.5, 0.25),
        "green_virt": normal_values(arg_keys[4], (NBF, NBF), NBF ** -0.5, 0.25),
    }


def images_of(blocks, index, green_occ, green_virt):
    count = blocks.shape[0]
    dense = jnp.zeros((count, NB * NB, BB), blocks.dtype).at[:, index].set(blocks)
    dense = dense.reshape(count, NB, NB, BLK, BLK).transpose(0, 1, 3, 2, 4).reshape(count, NBF, NBF)
    half = jnp.einsum("qms,ts->qmt", dense.astype(jnp.float32), green_virt.astype(jnp.float32)).astype(jnp.bfloat16)
    full = jnp.einsum("lm,qmt->qlt", green_occ.astype(jnp.float32), half.astype(jnp.float32)).astype(jnp.bfloat16)
    full = full.reshape(count, NB, BLK, NB, BLK).transpose(0, 1, 3, 2, 4).reshape(count, NB * NB, BB)
    return full[:, index]


def reference(tensor, pattern, pair_blocks, green_occ, green_virt):
    mask = jnp.repeat(pattern, RB, axis=1).astype(tensor.dtype)
    masked = tensor * mask[:, :, None]
    index = (pair_blocks[:, 0] * NB + pair_blocks[:, 1]).astype(jnp.int32)
    group = 8
    batches = masked.transpose(1, 0, 2).reshape(RI_W // group, group, NPAIRS, BB)
    images = lax.map(lambda blocks: images_of(blocks, index, green_occ, green_virt), batches)
    images = images.reshape(RI_W, NPAIRS * BB)
    left = masked.transpose(1, 0, 2).reshape(RI_W, NPAIRS * BB)
    return jnp.dot(left, images.T, preferred_element_type=jnp.float32)
```

```python
import jax
import jax.numpy as jnp
from jax import lax
from jax.experimental import pallas as pl
from jax.experimental.pallas import tpu as pltpu
from jax.sharding import PartitionSpec as P

BLK = 48
NB = 12
RB = 32
BB = 2304
NX, NY, NZ = 4, 4, 16
GROUPS = NX * NZ
MESH = pl.DeviceIdType.MESH
BF = jnp.bfloat16
F32 = jnp.float32


def nt(a, b):
    return lax.dot_general(a, b, (((1,), (1,)), ((), ())), preferred_element_type=F32)


def nn(a, b):
    return jnp.dot(a, b, preferred_element_type=F32)


def one_hot(rows, cols, match):
    r = lax.broadcasted_iota(jnp.int32, (rows, cols), 0)
    c = lax.broadcasted_iota(jnp.int32, (rows, cols), 1)
    return jnp.where(match(r, c), 1.0, 0.0).astype(BF)


def pad64(r, u):
    return (u == BLK * lax.div(r, 64) + lax.rem(r, 64)) & (lax.rem(r, 64) < BLK)


def pad80(r, u):
    return (u == 8 * lax.rem(r, 80) + lax.div(r, 80)) & (lax.rem(r, 80) < 72)


def by_q(r, c):
    q, w = lax.div(r, 80), lax.rem(r, 80)
    return (c == lax.div(w, 6) * 32 + q * 6 + lax.rem(w, 6)) & (w < 72)


def by_block(r, c):
    return by_q(c, r)


def by_m(r, c):
    mh, rest = lax.div(r, 32), lax.rem(r, 32)
    return c == rest * 6 + mh


def kernel(
    inv, pb, send1, dm, gv, go, out,
    recv1, dall, dense, xs, ys, ws, send2, recv2, img, xsend, xrecv, zsend, zrecv, fsend,
    gvp, gop, pa, pbk, pc,
    s1, r1, sy, ry, s2, r2, sx, rx, sz, rz, sf, rf, local,
):
    me = lax.axis_index("pair")
    ri = lax.axis_index("ri")
    x, z = lax.div(me, NZ), lax.rem(me, NZ)
    y, core = lax.div(ri, 2), lax.rem(ri, 2)
    sib = y * 2 + 1 - core
    up = lax.rem(y + 1, NY) * 2 + core
    down = lax.rem(y + NY - 1, NY) * 2 + core
    far = lax.rem(y + 2, NY) * 2 + core

    bar = pltpu.get_barrier_semaphore()

    def greet(pair, r):
        pl.semaphore_signal(bar, inc=1, device_id={"pair": pair, "ri": r}, device_id_type=MESH)

    def greet_pair(k, c):
        greet(lax.rem(me + k, GROUPS), ri)
        return c

    lax.fori_loop(1, GROUPS, greet_pair, 0)
    for k in range(NZ):
        greet(x * NZ + lax.rem(z + k, NZ), sib)
    greet(me, up)
    greet(me, down)

    @pl.when(x != y)
    def _():
        greet(y * NZ + z, x * 2 + core)

    pl.semaphore_wait(bar, GROUPS - 1 + NZ + 2 + jnp.where(x != y, 1, 0))

    def swap(src, dst, ss, rs, k):
        to = lax.rem(me + k, GROUPS)
        return pltpu.make_async_remote_copy(
            src_ref=src.at[to], dst_ref=dst.at[me], send_sem=ss.at[k], recv_sem=rs.at[me],
            device_id={"pair": to}, device_id_type=MESH,
        )

    def swapped(src, dst, ss, rs, k):
        fro = lax.rem(me + k, GROUPS)
        return pltpu.make_async_remote_copy(
            src_ref=src.at[fro], dst_ref=dst.at[fro], send_sem=ss.at[k], recv_sem=rs.at[fro],
            device_id={"pair": fro}, device_id_type=MESH,
        )

    def along(src, dst, i, to):
        return pltpu.make_async_remote_copy(
            src_ref=src, dst_ref=dst, send_sem=sy.at[i], recv_sem=ry.at[i],
            device_id={"ri": to}, device_id_type=MESH,
        )

    def start1(k, c):
        swap(send1, recv1, s1, r1, k).start()
        return c

    g_up = along(dm, dall.at[ri], 0, up)
    g_down = along(dm, dall.at[ri], 1, down)
    g_sib = along(dm, dall.at[ri], 2, sib)
    g_up.start()
    g_down.start()
    lax.fori_loop(1, GROUPS, start1, 0)
    g_sib.start()
    own1 = pltpu.make_async_copy(send1.at[me], recv1.at[me], local.at[0])
    own1.start()
    ownd = pltpu.make_async_copy(dm, dall.at[ri], local.at[1])
    ownd.start()
    recv1[GROUPS] = jnp.zeros((24, 384), BF)

    e = one_hot(768, 576, pad64)
    gvp[...] = nt(nt(e, gv[...]).astype(BF), e).astype(BF)
    f = one_hot(640, 576, pad80)
    gop[...] = nt(nn(f, go[...]).astype(BF), f).astype(BF)
    pa[...] = one_hot(320, 384, by_q)
    pbk[...] = one_hot(384, 320, by_block)
    pc[...] = one_hot(192, 192, by_m)

    half = pl.ds(0, 128)
    rest = pl.ds(128, 128)
    along(dm, dall.at[down], 0, up).wait_recv()
    h_up = along(dall.at[down, half], dall.at[down, half], 3, up)
    h_up.start()
    f_down = along(dall.at[down], dall.at[down], 4, sib)
    f_down.start()
    along(dm, dall.at[up], 1, down).wait_recv()
    h_down = along(dall.at[up, rest], dall.at[up, rest], 5, down)
    h_down.start()
    f_up = along(dall.at[up], dall.at[up], 6, sib)
    f_up.start()

    own1.wait()

    def end1(k, c):
        swapped(send1, recv1, s1, r1, k).wait()
        return c

    lax.fori_loop(1, GROUPS, end1, 0)

    def place(n, c):
        i, jp = lax.div(n, 6), lax.rem(n, 6)
        lowr = jnp.zeros((8, 384), BF)
        b0 = jnp.concatenate([recv1[inv[2 * n]], lowr], axis=0)
        b1 = jnp.concatenate([recv1[inv[2 * n + 1]], lowr], axis=0)
        gap = jnp.zeros((32, 16), BF)
        low = jnp.zeros((8, 128), BF)
        for a in range(8):
            cut = slice(a * BLK, (a + 1) * BLK)
            row = jnp.concatenate([b0[:, cut], gap, b1[:, cut], gap], axis=1)
            dense[a, jp, i] = row
        return c

    lax.fori_loop(0, 72, place, 0)

    def first(a, c):
        d = jnp.concatenate([dense[a, jp].reshape(384, 128) for jp in range(6)], axis=1)
        d = nn(pa[...], d).astype(BF)
        h = nn(d, gvp[...]).astype(BF)
        for q in range(4):
            xs[q, a] = h[q * 80 : (q + 1) * 80]
        return c

    lax.fori_loop(0, 8, first, 0)

    def second(q, c):
        v = nn(gop[...], xs[q].reshape(640, 768)).astype(BF)
        for a in range(8):
            ys[a, q] = v[a * 80 : (a + 1) * 80]
        return c

    lax.fori_loop(0, 4, second, 0)

    def third(a, c):
        v = nn(pbk[...], ys[a].reshape(320, 768)).astype(BF)
        for tp in range(6):
            ws[a, tp] = v[:, tp * 128 : (tp + 1) * 128].reshape(12, 32, 128)
        return c

    lax.fori_loop(0, 8, third, 0)

    def pack(p):
        l, t = pb[2 * p], pb[2 * p + 1]
        tp, odd = lax.div(t, 2), lax.rem(t, 2)
        cols = []
        for a in range(8):
            w = ws[a, tp, l]
            cols.append(jnp.where(odd == 1, w[:24, 64:112], w[:24, 0:48]))
        send2[p] = jnp.concatenate(cols, axis=1)

    def start2(k, c):
        pack(lax.rem(me + k, GROUPS))
        swap(send2, recv2, s2, r2, k).start()
        return c

    lax.fori_loop(1, GROUPS, start2, 0)
    pack(me)
    own2 = pltpu.make_async_copy(send2.at[me], recv2.at[me], local.at[2])
    own2.start()

    along(dm.at[half], dall.at[far, half], 3, up).wait_recv()
    along(dm.at[rest], dall.at[far, rest], 5, down).wait_recv()
    f_far = along(dall.at[far], dall.at[far], 7, sib)
    f_far.start()
    ownd.wait()
    g_sib.wait_recv()
    f_down.wait_recv()
    f_up.wait_recv()
    f_far.wait_recv()
    own2.wait()

    def end2(k, c):
        swapped(send2, recv2, s2, r2, k).wait()
        return c

    lax.fori_loop(1, GROUPS, end2, 0)

    for g in range(8):
        v = nn(pc[...], recv2[g * 8 : (g + 1) * 8].reshape(192, 384)).astype(BF)
        for mh in range(6):
            img[g * 32 : (g + 1) * 32, mh * 384 : (mh + 1) * 384] = v[mh * 32 : (mh + 1) * 32]

    def part(xt):
        return jnp.concatenate([nt(img[...], dall[2 * xt]), nt(img[...], dall[2 * xt + 1])], axis=1)

    def across(k):
        return pltpu.make_async_remote_copy(
            src_ref=xsend.at[k], dst_ref=xrecv.at[k], send_sem=sx.at[k], recv_sem=rx.at[k],
            device_id={"pair": lax.rem(x + k + 1, NX) * NZ + z}, device_id_type=MESH,
        )

    for k in (1, 0, 2):
        xsend[k] = part(lax.rem(x + k + 1, NX)).astype(BF)
        across(k).start()
    total = part(x)
    for k in (1, 0, 2):
        across(k).wait()
        total = total + xrecv[k].astype(F32)
    total = total.astype(BF)
    for h in range(2):
        for q in range(8):
            zsend[q, h] = total[q * 32 : (q + 1) * 32, h * 256 : (h + 1) * 256]

    def deal(q, h):
        return pltpu.make_async_remote_copy(
            src_ref=zsend.at[q, h], dst_ref=zrecv.at[z], send_sem=sz.at[q, h], recv_sem=rz.at[z],
            device_id={"pair": x * NZ + core * 8 + q, "ri": y * 2 + h}, device_id_type=MESH,
        )

    def dealt(fro):
        return pltpu.make_async_remote_copy(
            src_ref=zsend.at[0, 0], dst_ref=zrecv.at[fro], send_sem=sz.at[0, 0],
            recv_sem=rz.at[fro], device_id={"pair": x * NZ + fro, "ri": ri}, device_id_type=MESH,
        )

    mine = lax.div(z, 8) == core
    zq = lax.rem(z, 8)
    for step in range(8):
        q = lax.rem(zq + step, 8)
        for h in range(2):
            if step == 0:
                same = mine & (core == h)

                @pl.when(same)
                def _():
                    pltpu.make_async_copy(zsend.at[q, h], zrecv.at[z], local.at[3]).start()

                @pl.when(jnp.logical_not(same))
                def _():
                    deal(q, h).start()
            else:
                deal(q, h).start()
    for step in range(8):
        q = lax.rem(zq + step, 8)
        for h in range(2):
            if step == 0:
                same = mine & (core == h)

                @pl.when(jnp.logical_not(same))
                def _():
                    deal(q, h).wait_send()
            else:
                deal(q, h).wait_send()

    @pl.when(mine)
    def _():
        pltpu.make_async_copy(zsend.at[0, 0], zrecv.at[z], local.at[3]).wait()

    @pl.when(jnp.logical_not(mine))
    def _():
        dealt(z).wait_recv()

    def end3(k, c):
        dealt(lax.rem(z + k, NZ)).wait_recv()
        return c

    lax.fori_loop(1, NZ, end3, 0)
    result = zrecv[0].astype(F32)
    for k in range(1, NZ):
        result = result + zrecv[k].astype(F32)

    @pl.when(x == y)
    def _():
        out[...] = result

    @pl.when(x != y)
    def _():
        fsend[...] = result
        turn = pltpu.make_async_remote_copy(
            src_ref=fsend, dst_ref=out, send_sem=sf, recv_sem=rf,
            device_id={"pair": y * NZ + z, "ri": x * 2 + core}, device_id_type=MESH,
        )
        turn.start()
        turn.wait()

    g_up.wait_send()
    g_down.wait_send()
    g_sib.wait_send()
    h_up.wait_send()
    h_down.wait_send()
    f_down.wait_send()
    f_up.wait_send()
    f_far.wait_send()


def on_device(tensor, pattern, pair_blocks, green_occ, green_virt):
    mask = jnp.repeat(pattern, RB, axis=1).astype(tensor.dtype)
    masked = (tensor * mask[:, :, None])[0]
    index = pair_blocks[:, 0] * NB + pair_blocks[:, 1]
    hits = index[None, :] == jnp.arange(NB * NB, dtype=jnp.int32)[:, None]
    order = jnp.arange(GROUPS, dtype=jnp.int32)[None, :]
    inverse = jnp.min(jnp.where(hits, order, GROUPS), axis=1).astype(jnp.int32)
    vmem = pl.BlockSpec(memory_space=pltpu.VMEM)
    smem = pl.BlockSpec(memory_space=pltpu.SMEM)
    dma = pltpu.SemaphoreType.DMA
    chi = pl.pallas_call(
        kernel,
        out_shape=jax.ShapeDtypeStruct((32, 256), F32),
        in_specs=[smem, smem, vmem, vmem, vmem, vmem],
        out_specs=vmem,
        scratch_shapes=[
            pltpu.VMEM((GROUPS + 1, 24, 384), BF),
            pltpu.VMEM((8, 256, BB), BF),
            pltpu.VMEM((8, 6, 12, 32, 128), BF),
            pltpu.VMEM((4, 8, 80, 768), BF),
            pltpu.VMEM((8, 4, 80, 768), BF),
            pltpu.VMEM((8, 6, 12, 32, 128), BF),
            pltpu.VMEM((GROUPS, 24, 384), BF),
            pltpu.VMEM((GROUPS, 24, 384), BF),
            pltpu.VMEM((256, BB), BF),
            pltpu.VMEM((3, 256, 512), BF),
            pltpu.VMEM((3, 256, 512), BF),
            pltpu.VMEM((8, 2, 32, 256), BF),
            pltpu.VMEM((NZ, 32, 256), BF),
            pltpu.VMEM((32, 256), F32),
            pltpu.VMEM((768, 768), BF),
            pltpu.VMEM((640, 640), BF),
            pltpu.VMEM((320, 384), BF),
            pltpu.VMEM((384, 320), BF),
            pltpu.VMEM((192, 192), BF),
            dma((GROUPS,)), dma((GROUPS,)),
            dma((8,)), dma((8,)),
            dma((GROUPS,)), dma((GROUPS,)),
            dma((3,)), dma((3,)),
            dma((8, 2)), dma((NZ,)),
            dma, dma,
            dma((4,)),
        ],
        compiler_params=pltpu.CompilerParams(
            collective_id=0, has_side_effects=True, vmem_limit_bytes=60 << 20
        ),
    )(inverse, pair_blocks.reshape(-1), masked.reshape(GROUPS, 24, 384), masked, green_virt, green_occ)
    return chi.T


def solution(mesh):
    in_specs = (P("pair", "ri", None), P("pair", "ri"), P(), P(), P())
    out_specs = P("ri", "pair")
    return jax.shard_map(
        on_device, mesh=mesh, in_specs=in_specs, out_specs=out_specs, check_vma=False
    )
```

```python
import jax
import jax.numpy as jnp
from jax import lax
from jax.experimental import pallas as pl
from jax.experimental.pallas import tpu as pltpu
from jax.sharding import PartitionSpec as P

BLK = 48
NB = 12
RB = 32
BB = 2304
NX, NY, NZ = 4, 4, 16
GROUPS = NX * NZ
TURNS = 2
SHARE = GROUPS // TURNS
ZT = NZ // TURNS
ZROWS = 32 // TURNS
MESH = pl.DeviceIdType.MESH
BF = jnp.bfloat16
F32 = jnp.float32


def nt(a, b):
    return lax.dot_general(a, b, (((1,), (1,)), ((), ())), preferred_element_type=F32)


def nn(a, b):
    return jnp.dot(a, b, preferred_element_type=F32)


def one_hot(rows, cols, match):
    r = lax.broadcasted_iota(jnp.int32, (rows, cols), 0)
    c = lax.broadcasted_iota(jnp.int32, (rows, cols), 1)
    return jnp.where(match(r, c), 1.0, 0.0).astype(BF)


def pad64(r, u):
    return (u == BLK * lax.div(r, 64) + lax.rem(r, 64)) & (lax.rem(r, 64) < BLK)


def pad80(r, u):
    return (u == 8 * lax.rem(r, 80) + lax.div(r, 80)) & (lax.rem(r, 80) < 72)


def by_q(r, c):
    q, w = lax.div(r, 80), lax.rem(r, 80)
    return (c == lax.div(w, 6) * 32 + q * 6 + lax.rem(w, 6)) & (w < 72)


def by_block(r, c):
    return by_q(c, r)


def from_m(r, c):
    return by_m(c, r)


def by_m(r, c):
    mh, rest = lax.div(r, 32), lax.rem(r, 32)
    return c == rest * 6 + mh


def kernel(
    inv, pb, pattern, tensor, gv, go, out,
    send1, dm, recv1, dall, dense, xs, ys, ws, send2, recv2, img, xsend, xrecv, zsend, zrecv, fsend,
    gvp, gop, pa, pbk, pc,
    s1, r1, sy, ry, s2, r2, sx, rx, sz, rz, sf, rf, local,
):
    me = lax.axis_index("pair")
    ri = lax.axis_index("ri")
    x, z = lax.div(me, NZ), lax.rem(me, NZ)
    y, core = lax.div(ri, 2), lax.rem(ri, 2)
    sib = y * 2 + 1 - core
    up = lax.rem(y + 1, NY) * 2 + core
    down = lax.rem(y + NY - 1, NY) * 2 + core
    far = lax.rem(y + 2, NY) * 2 + core

    bar = pltpu.get_barrier_semaphore()

    def greet(pair, r):
        pl.semaphore_signal(bar, inc=1, device_id={"pair": pair, "ri": r}, device_id_type=MESH)

    def greet_pair(k, c):
        greet(lax.rem(me + k, GROUPS), ri)
        return c

    lax.fori_loop(1, GROUPS, greet_pair, 0)
    for k in range(NZ):
        greet(x * NZ + lax.rem(z + k, NZ), sib)
    greet(me, up)
    greet(me, down)

    @pl.when(x != y)
    def _():
        greet(y * NZ + z, x * 2 + core)

    pc[...] = one_hot(192, 192, from_m)
    for g in range(8):
        rows = slice(g * RB, (g + 1) * RB)
        masked = tensor[0, rows] * pattern[0, g].astype(BF)
        dm[rows] = masked
        v = jnp.concatenate([masked[:, m * 384 : (m + 1) * 384] for m in range(6)], axis=0)
        send1[g * 8 : (g + 1) * 8] = nn(pc[...], v).astype(BF).reshape(8, 24, 384)

    pl.semaphore_wait(bar, GROUPS - 1 + NZ + 2 + jnp.where(x != y, 1, 0))

    def along(src, dst, i, to):
        return pltpu.make_async_remote_copy(
            src_ref=src, dst_ref=dst, send_sem=sy.at[i], recv_sem=ry.at[i],
            device_id={"ri": to}, device_id_type=MESH,
        )

    def nth(n):
        turn, rest = lax.div(n, SHARE), lax.rem(n, SHARE)
        dx, dz = lax.div(rest, ZT), lax.rem(rest, ZT)
        return lax.rem(x + dx, NX) * NZ + lax.rem(lax.div(z, TURNS) + dz, ZT) * TURNS + turn

    def swap1(to):
        return pltpu.make_async_remote_copy(
            src_ref=send1.at[to], dst_ref=recv1.at[me], send_sem=s1.at[to], recv_sem=r1.at[me],
            device_id={"pair": to}, device_id_type=MESH,
        )

    def start1(n, c):
        to = nth(n)

        @pl.when(to != me)
        def _():
            swap1(to).start()

        return c

    g_up = along(dm, dall.at[ri], 0, up)
    g_down = along(dm, dall.at[ri], 1, down)
    g_sib = along(dm, dall.at[ri], 2, sib)
    lax.fori_loop(0, GROUPS, start1, 0)
    g_up.start()
    g_down.start()
    g_sib.start()
    own1 = pltpu.make_async_copy(send1.at[me], recv1.at[me], local.at[0])
    own1.start()
    ownd = pltpu.make_async_copy(dm, dall.at[ri], local.at[1])
    ownd.start()
    recv1[GROUPS] = jnp.zeros((24, 384), BF)

    e = one_hot(768, 576, pad64)
    gvp[...] = nt(nt(e, gv[...]).astype(BF), e).astype(BF)
    f = one_hot(640, 576, pad80)
    gop[...] = nt(nn(f, go[...]).astype(BF), f).astype(BF)
    pa[...] = one_hot(320, 384, by_q)
    pbk[...] = one_hot(384, 320, by_block)
    pc[...] = one_hot(192, 192, by_m)

    half = pl.ds(0, 128)
    rest = pl.ds(128, 128)
    along(dm, dall.at[down], 0, up).wait_recv()
    h_up = along(dall.at[down, half], dall.at[down, half], 3, up)
    h_up.start()
    f_down = along(dall.at[down], dall.at[down], 4, sib)
    f_down.start()
    along(dm, dall.at[up], 1, down).wait_recv()
    h_down = along(dall.at[up, rest], dall.at[up, rest], 5, down)
    h_down.start()
    f_up = along(dall.at[up], dall.at[up], 6, sib)
    f_up.start()

    own1.wait()

    def end1(k, c):
        fro = lax.rem(me + k, GROUPS)
        pltpu.make_async_remote_copy(
            src_ref=send1.at[fro], dst_ref=recv1.at[fro], send_sem=s1.at[fro],
            recv_sem=r1.at[fro], device_id={"pair": fro}, device_id_type=MESH,
        ).wait()
        return c

    lax.fori_loop(1, GROUPS, end1, 0)

    def place(n, c):
        i, jp = lax.div(n, 6), lax.rem(n, 6)
        lowr = jnp.zeros((8, 384), BF)
        b0 = jnp.concatenate([recv1[inv[2 * n]], lowr], axis=0)
        b1 = jnp.concatenate([recv1[inv[2 * n + 1]], lowr], axis=0)
        gap = jnp.zeros((32, 16), BF)
        low = jnp.zeros((8, 128), BF)
        for a in range(8):
            cut = slice(a * BLK, (a + 1) * BLK)
            row = jnp.concatenate([b0[:, cut], gap, b1[:, cut], gap], axis=1)
            dense[a, jp, i] = row
        return c

    lax.fori_loop(0, 72, place, 0)

    def first(a, c):
        d = jnp.concatenate([dense[a, jp].reshape(384, 128) for jp in range(6)], axis=1)
        d = nn(pa[...], d).astype(BF)
        h = nn(d, gvp[...]).astype(BF)
        for q in range(4):
            xs[q, a] = h[q * 80 : (q + 1) * 80]
        return c

    lax.fori_loop(0, 8, first, 0)

    def second(q, c):
        v = nn(gop[...], xs[q].reshape(640, 768)).astype(BF)
        for a in range(8):
            ys[a, q] = v[a * 80 : (a + 1) * 80]
        return c

    lax.fori_loop(0, 4, second, 0)

    def third(a, c):
        v = nn(pbk[...], ys[a].reshape(320, 768)).astype(BF)
        for tp in range(6):
            ws[a, tp] = v[:, tp * 128 : (tp + 1) * 128].reshape(12, 32, 128)
        return c

    lax.fori_loop(0, 8, third, 0)

    def pack(p):
        l, t = pb[0, p], pb[1, p]
        tp, odd = lax.div(t, 2), lax.rem(t, 2)
        cols = []
        for a in range(8):
            w = ws[a, tp, l]
            cols.append(jnp.where(odd == 1, w[:24, 64:112], w[:24, 0:48]))
        send2[p] = jnp.concatenate(cols, axis=1)

    def slot(pair):
        w = lax.rem(pair, NZ)
        return lax.rem(w, TURNS) * SHARE + lax.div(pair, NZ) * ZT + lax.div(w, TURNS)

    def swap2(to):
        return pltpu.make_async_remote_copy(
            src_ref=send2.at[to], dst_ref=recv2.at[slot(me)], send_sem=s2.at[to],
            recv_sem=r2.at[slot(me)], device_id={"pair": to}, device_id_type=MESH,
        )

    def start2(k, c):
        to = lax.rem(me + k, GROUPS)
        pack(to)
        swap2(to).start()
        return c

    lax.fori_loop(1, GROUPS, start2, 0)
    pack(me)
    own2 = pltpu.make_async_copy(send2.at[me], recv2.at[slot(me)], local.at[2])
    own2.start()

    along(dm.at[half], dall.at[far, half], 3, up).wait_recv()
    along(dm.at[rest], dall.at[far, rest], 5, down).wait_recv()
    f_far = along(dall.at[far], dall.at[far], 7, sib)
    f_far.start()
    ownd.wait()
    g_sib.wait_recv()
    f_down.wait_recv()
    f_up.wait_recv()
    f_far.wait_recv()

    def part(xt):
        return jnp.concatenate([nt(img[...], dall[2 * xt]), nt(img[...], dall[2 * xt + 1])], axis=1)

    def across(turn, k):
        return pltpu.make_async_remote_copy(
            src_ref=xsend.at[turn, k], dst_ref=xrecv.at[turn, k], send_sem=sx.at[turn, k],
            recv_sem=rx.at[turn, k], device_id={"pair": lax.rem(x + k + 1, NX) * NZ + z},
            device_id_type=MESH,
        )

    def deal(turn, q, h):
        return pltpu.make_async_remote_copy(
            src_ref=zsend.at[turn, q, h], dst_ref=zrecv.at[turn, z], send_sem=sz.at[turn, q, h],
            recv_sem=rz.at[turn, z],
            device_id={"pair": x * NZ + core * 8 + q, "ri": y * 2 + h}, device_id_type=MESH,
        )

    mine = lax.div(z, 8) == core
    zq = lax.rem(z, 8)

    def kept(turn):
        return pltpu.make_async_copy(zsend.at[turn, zq, core], zrecv.at[turn, z], local.at[3 + turn])

    def each(turn, do):
        for step in range(8):
            q = lax.rem(zq + step, 8)
            for h in range(2):
                if step == 0:

                    @pl.when(jnp.logical_not(mine & (core == h)))
                    def _():
                        do(deal(turn, q, h))
                else:
                    do(deal(turn, q, h))

    for turn in range(TURNS):

        @pl.when(lax.rem(z, TURNS) == turn)
        def _():
            own2.wait()

        def arrive(n, c):
            at = turn * SHARE + n

            @pl.when(at != slot(me))
            def _():
                pltpu.make_async_remote_copy(
                    src_ref=send2.at[0], dst_ref=recv2.at[at], send_sem=s2.at[0],
                    recv_sem=r2.at[at], device_id={"pair": me}, device_id_type=MESH,
                ).wait_recv()

            return c

        lax.fori_loop(0, SHARE, arrive, 0)
        for g in range(SHARE // 8):
            at = turn * SHARE + g * 8
            v = nn(pc[...], recv2[at : at + 8].reshape(192, 384)).astype(BF)
            for mh in range(6):
                img[g * 32 : (g + 1) * 32, mh * 384 : (mh + 1) * 384] = v[mh * 32 : (mh + 1) * 32]
        for k in (1, 0, 2):
            xsend[turn, k] = part(lax.rem(x + k + 1, NX)).astype(BF)
            across(turn, k).start()
        total = part(x)
        for k in (1, 0, 2):
            across(turn, k).wait()
            total = total + xrecv[turn, k].astype(F32)
        total = total.astype(BF)
        for h in range(2):
            for q in range(8):
                zsend[turn, q, h] = total[q * ZROWS : (q + 1) * ZROWS, h * 256 : (h + 1) * 256]
        each(turn, lambda copy: copy.start())

        @pl.when(mine)
        def _():
            kept(turn).start()

    for turn in range(TURNS):
        each(turn, lambda copy: copy.wait_send())

        def dealt(fro):
            return pltpu.make_async_remote_copy(
                src_ref=zsend.at[0, 0, 0], dst_ref=zrecv.at[turn, fro], send_sem=sz.at[0, 0, 0],
                recv_sem=rz.at[turn, fro], device_id={"pair": me}, device_id_type=MESH,
            )

        @pl.when(mine)
        def _():
            kept(turn).wait()

        @pl.when(jnp.logical_not(mine))
        def _():
            dealt(z).wait_recv()

        def end3(k, c):
            dealt(lax.rem(z + k, NZ)).wait_recv()
            return c

        lax.fori_loop(1, NZ, end3, 0)
        some = zrecv[turn, 0].astype(F32)
        for k in range(1, NZ):
            some = some + zrecv[turn, k].astype(F32)
        for j in range(8 // TURNS):
            at = (j * TURNS + turn) * 4
            fsend[at : at + 4] = some[j * 4 : j * 4 + 4]

    @pl.when(x == y)
    def _():
        out[...] = fsend[...]

    @pl.when(x != y)
    def _():
        turn = pltpu.make_async_remote_copy(
            src_ref=fsend, dst_ref=out, send_sem=sf, recv_sem=rf,
            device_id={"pair": y * NZ + z, "ri": x * 2 + core}, device_id_type=MESH,
        )
        turn.start()
        turn.wait()

    def sent2(k, c):
        swap2(lax.rem(me + k, GROUPS)).wait_send()
        return c

    lax.fori_loop(1, GROUPS, sent2, 0)
    g_up.wait_send()
    g_down.wait_send()
    g_sib.wait_send()
    h_up.wait_send()
    h_down.wait_send()
    f_down.wait_send()
    f_up.wait_send()
    f_far.wait_send()


def on_device(tensor, pattern, pair_blocks, green_occ, green_virt):
    index = pair_blocks[:, 0] * NB + pair_blocks[:, 1]
    hits = index[None, :] == jnp.arange(NB * NB, dtype=jnp.int32)[:, None]
    order = jnp.arange(GROUPS, dtype=jnp.int32)[None, :]
    inverse = jnp.min(jnp.where(hits, order, GROUPS), axis=1).astype(jnp.int32)
    vmem = pl.BlockSpec(memory_space=pltpu.VMEM)
    smem = pl.BlockSpec(memory_space=pltpu.SMEM)
    dma = pltpu.SemaphoreType.DMA
    chi = pl.pallas_call(
        kernel,
        out_shape=jax.ShapeDtypeStruct((32, 256), F32),
        in_specs=[smem, smem, smem, vmem, vmem, vmem],
        out_specs=vmem,
        scratch_shapes=[
            pltpu.VMEM((GROUPS, 24, 384), BF),
            pltpu.VMEM((256, BB), BF),
            pltpu.VMEM((GROUPS + 1, 24, 384), BF),
            pltpu.VMEM((8, 256, BB), BF),
            pltpu.VMEM((8, 6, 12, 32, 128), BF),
            pltpu.VMEM((4, 8, 80, 768), BF),
            pltpu.VMEM((8, 4, 80, 768), BF),
            pltpu.VMEM((8, 6, 12, 32, 128), BF),
            pltpu.VMEM((GROUPS, 24, 384), BF),
            pltpu.VMEM((GROUPS, 24, 384), BF),
            pltpu.VMEM((SHARE * 4, BB), BF),
            pltpu.VMEM((TURNS, 3, SHARE * 4, 512), BF),
            pltpu.VMEM((TURNS, 3, SHARE * 4, 512), BF),
            pltpu.VMEM((TURNS, 8, 2, ZROWS, 256), BF),
            pltpu.VMEM((TURNS, NZ, ZROWS, 256), BF),
            pltpu.VMEM((32, 256), F32),
            pltpu.VMEM((768, 768), BF),
            pltpu.VMEM((640, 640), BF),
            pltpu.VMEM((320, 384), BF),
            pltpu.VMEM((384, 320), BF),
            pltpu.VMEM((192, 192), BF),
            dma((GROUPS,)), dma((GROUPS,)),
            dma((8,)), dma((8,)),
            dma((GROUPS,)), dma((GROUPS,)),
            dma((TURNS, 3)), dma((TURNS, 3)),
            dma((TURNS, 8, 2)), dma((TURNS, NZ)),
            dma, dma,
            dma((3 + TURNS,)),
        ],
        compiler_params=pltpu.CompilerParams(
            collective_id=0, has_side_effects=True, vmem_limit_bytes=60 << 20
        ),
    )(inverse, pair_blocks.T, pattern, tensor, green_virt, green_occ)
    return chi.T


def solution(mesh):
    in_specs = (P("pair", "ri", None), P("pair", "ri"), P(), P(), P())
    out_specs = P("ri", "pair")
    return jax.shard_map(
        on_device, mesh=mesh, in_specs=in_specs, out_specs=out_specs, check_vma=False
    )
```

```python
import jax
import jax.numpy as jnp
from jax import lax
from jax.experimental import pallas as pl
from jax.experimental.pallas import tpu as pltpu
from jax.sharding import PartitionSpec as P

BLK = 48
NB = 12
RB = 32
BB = 2304
NX, NY, NZ = 4, 4, 16
GROUPS = NX * NZ
TURNS = 2
SHARE = GROUPS // TURNS
ZT = NZ // TURNS
ZROWS = 32 // TURNS
MESH = pl.DeviceIdType.MESH
BF = jnp.bfloat16
F32 = jnp.float32


def nt(a, b):
    return lax.dot_general(a, b, (((1,), (1,)), ((), ())), preferred_element_type=F32)


def nn(a, b):
    return jnp.dot(a, b, preferred_element_type=F32)


def one_hot(rows, cols, match):
    r = lax.broadcasted_iota(jnp.int32, (rows, cols), 0)
    c = lax.broadcasted_iota(jnp.int32, (rows, cols), 1)
    return jnp.where(match(r, c), 1.0, 0.0).astype(BF)


def pad64(r, u):
    return (u == BLK * lax.div(r, 64) + lax.rem(r, 64)) & (lax.rem(r, 64) < BLK)


def pad32(r, u):
    b, w = lax.div(r, 384), lax.rem(r, 384)
    return (u == BLK * lax.div(w, 32) + 2 * lax.rem(w, 32) + b) & (lax.rem(w, 32) < 24)


def to_slab(r, c):
    d, w = lax.div(c, 192), lax.rem(c, 192)
    q = lax.rem(w, 4)
    at = lax.div(lax.rem(w, 32), 4) * 24 + lax.div(w, 32) * 4
    return r == at + lax.rem(q + 4 - d, 4)


def from_slab(r, c):
    d, w = lax.div(c, 192), lax.rem(c, 192)
    g, mh, rr = lax.div(w, 24), lax.div(lax.rem(w, 24), 4), lax.rem(w, 4)
    return r == mh * 32 + g * 4 + lax.rem(rr + d, 4)


def shifted(v, sign):
    row = lax.broadcasted_iota(jnp.int32, v.shape, 0)
    lane = lax.broadcasted_iota(jnp.int32, v.shape, 1)
    keep = lax.rem(row, 4) == lax.div(lane, 96)
    zero = jnp.zeros_like(v)
    rolled = [v] + [pltpu.roll(v, (sign * 96 * d) % 384, 1) for d in (1, 2, 3)]
    return jnp.concatenate([jnp.where(keep, u, zero) for u in rolled], axis=0)


def kernel(
    inv, pb, pattern, tensor, gv, go, out,
    send1, dm, recv1, dall, dense, ws, send2, recv2, img, xsend, xrecv, zsend, zrecv, fsend,
    gvp, gop, pc,
    s1, r1, sy, ry, s2, r2, sx, rx, sz, rz, sf, rf, local,
):
    me = lax.axis_index("pair")
    ri = lax.axis_index("ri")
    x, z = lax.div(me, NZ), lax.rem(me, NZ)
    y, core = lax.div(ri, 2), lax.rem(ri, 2)
    sib = y * 2 + 1 - core
    up = lax.rem(y + 1, NY) * 2 + core
    down = lax.rem(y + NY - 1, NY) * 2 + core
    far = lax.rem(y + 2, NY) * 2 + core

    bar = pltpu.get_barrier_semaphore()

    def greet(pair, r):
        pl.semaphore_signal(bar, inc=1, device_id={"pair": pair, "ri": r}, device_id_type=MESH)

    def greet_pair(k, c):
        greet(lax.rem(me + k, GROUPS), ri)
        return c

    lax.fori_loop(1, GROUPS, greet_pair, 0)
    for k in range(NZ):
        greet(x * NZ + lax.rem(z + k, NZ), sib)
    greet(me, up)
    greet(me, down)

    @pl.when(x != y)
    def _():
        greet(y * NZ + z, x * 2 + core)

    pc[...] = one_hot(192, 768, to_slab)
    for g in range(8):
        rows = slice(g * RB, (g + 1) * RB)
        masked = tensor[0, rows] * pattern[0, g].astype(BF)
        dm[rows] = masked
        v = jnp.concatenate([masked[:, m * 384 : (m + 1) * 384] for m in range(6)], axis=0)
        send1[g * 8 : (g + 1) * 8] = nn(pc[...], shifted(v, 1)).astype(BF).reshape(8, 24, 384)

    pl.semaphore_wait(bar, GROUPS - 1 + NZ + 2 + jnp.where(x != y, 1, 0))

    def along(src, dst, i, to):
        return pltpu.make_async_remote_copy(
            src_ref=src, dst_ref=dst, send_sem=sy.at[i], recv_sem=ry.at[i],
            device_id={"ri": to}, device_id_type=MESH,
        )

    def nth(n):
        turn, rest = lax.div(n, SHARE), lax.rem(n, SHARE)
        dx, dz = lax.div(rest, ZT), lax.rem(rest, ZT)
        return lax.rem(x + dx, NX) * NZ + lax.rem(lax.div(z, TURNS) + dz, ZT) * TURNS + turn

    def swap1(to):
        return pltpu.make_async_remote_copy(
            src_ref=send1.at[to], dst_ref=recv1.at[me], send_sem=s1.at[to], recv_sem=r1.at[me],
            device_id={"pair": to}, device_id_type=MESH,
        )

    def start1(n, c):
        to = nth(n)

        @pl.when(to != me)
        def _():
            swap1(to).start()

        return c

    g_up = along(dm, dall.at[ri], 0, up)
    g_down = along(dm, dall.at[ri], 1, down)
    g_sib = along(dm, dall.at[ri], 2, sib)
    lax.fori_loop(0, GROUPS, start1, 0)
    g_up.start()
    g_down.start()
    g_sib.start()
    own1 = pltpu.make_async_copy(send1.at[me], recv1.at[me], local.at[0])
    own1.start()
    ownd = pltpu.make_async_copy(dm, dall.at[ri], local.at[1])
    ownd.start()
    recv1[GROUPS] = jnp.zeros((24, 384), BF)

    e = one_hot(768, 576, pad64)
    gvp[...] = nt(nt(e, gv[...]).astype(BF), e).astype(BF)
    f = one_hot(768, 576, pad32)
    gop[...] = nt(nn(f, go[...]).astype(BF), f).astype(BF)
    pc[...] = one_hot(192, 768, from_slab)

    half = pl.ds(0, 128)
    rest = pl.ds(128, 128)
    along(dm, dall.at[down], 0, up).wait_recv()
    h_up = along(dall.at[down, half], dall.at[down, half], 3, up)
    h_up.start()
    f_down = along(dall.at[down], dall.at[down], 4, sib)
    f_down.start()
    along(dm, dall.at[up], 1, down).wait_recv()
    h_down = along(dall.at[up, rest], dall.at[up, rest], 5, down)
    h_down.start()
    f_up = along(dall.at[up], dall.at[up], 6, sib)
    f_up.start()

    own1.wait()

    def end1(k, c):
        fro = lax.rem(me + k, GROUPS)
        pltpu.make_async_remote_copy(
            src_ref=send1.at[fro], dst_ref=recv1.at[fro], send_sem=s1.at[fro],
            recv_sem=r1.at[fro], device_id={"pair": fro}, device_id_type=MESH,
        ).wait()
        return c

    lax.fori_loop(1, GROUPS, end1, 0)

    lane = lax.broadcasted_iota(jnp.int32, (32, 128), 1)

    def cut(tiles, n, at):
        t, low = n * BLK // 128, n * BLK % 128
        piece = pltpu.roll(tiles[t], (at - low) % 128, 1)
        if low + BLK > 128:
            more = pltpu.roll(tiles[t + 1], (at - low) % 128, 1)
            piece = jnp.where(lane < at + 128 - low, piece, more)
        return piece

    def place(n, c):
        i, jp = lax.div(n, 6), lax.rem(n, 6)
        low = jnp.zeros((8, 128), BF)

        def tiles(p):
            return [
                jnp.concatenate([recv1[p, :, t * 128 : (t + 1) * 128], low], axis=0)
                for t in range(3)
            ]

        b0, b1 = tiles(inv[2 * n]), tiles(inv[2 * n + 1])
        for a in range(8):
            dense[a // 2, jp, a % 2, i] = jnp.where(lane < 64, cut(b0, a, 0), cut(b1, a, 64))
        return c

    lax.fori_loop(0, 72, place, 0)

    def image(q, c):
        d = jnp.concatenate([dense[q, jp].reshape(768, 128) for jp in range(6)], axis=1)
        h = nn(d, gvp[...]).astype(BF)
        v = nn(gop[...], h).astype(BF)
        for tp in range(6):
            ws[q, tp] = v[:, tp * 128 : (tp + 1) * 128].reshape(2, 12, 32, 128)
        return c

    lax.fori_loop(0, 4, image, 0)

    def pack(p):
        l, t = pb[0, p], pb[1, p]
        tp, odd = lax.div(t, 2), lax.rem(t, 2)
        rolled = []
        for a in range(8):
            w = ws[a // 2, tp, a % 2, l]
            at = a * BLK % 128
            rolled.append(jnp.where(odd == 1, pltpu.roll(w, (at + 64) % 128, 1), pltpu.roll(w, at, 1)))
        for t in range(3):
            out_tile = None
            for a in reversed(range(8)):
                first, last = a * BLK - t * 128, (a + 1) * BLK - t * 128
                if last > 0 and first < 128:
                    if out_tile is None:
                        out_tile = rolled[a]
                    else:
                        out_tile = jnp.where(lane < last, rolled[a], out_tile)
            send2[p, :, t * 128 : (t + 1) * 128] = out_tile[:24]

    def slot(pair):
        w = lax.rem(pair, NZ)
        return lax.rem(w, TURNS) * SHARE + lax.div(pair, NZ) * ZT + lax.div(w, TURNS)

    def swap2(to):
        return pltpu.make_async_remote_copy(
            src_ref=send2.at[to], dst_ref=recv2.at[slot(me)], send_sem=s2.at[to],
            recv_sem=r2.at[slot(me)], device_id={"pair": to}, device_id_type=MESH,
        )

    def start2(k, c):
        to = lax.rem(me + k, GROUPS)
        pack(to)
        swap2(to).start()
        return c

    lax.fori_loop(1, GROUPS, start2, 0)
    pack(me)
    own2 = pltpu.make_async_copy(send2.at[me], recv2.at[slot(me)], local.at[2])
    own2.start()

    along(dm.at[half], dall.at[far, half], 3, up).wait_recv()
    along(dm.at[rest], dall.at[far, rest], 5, down).wait_recv()
    f_far = along(dall.at[far], dall.at[far], 7, sib)
    f_far.start()
    ownd.wait()
    g_sib.wait_recv()
    f_down.wait_recv()
    f_up.wait_recv()
    f_far.wait_recv()

    def part(xt):
        return jnp.concatenate([nt(img[...], dall[2 * xt]), nt(img[...], dall[2 * xt + 1])], axis=1)

    def across(turn, k):
        return pltpu.make_async_remote_copy(
            src_ref=xsend.at[turn, k], dst_ref=xrecv.at[turn, k], send_sem=sx.at[turn, k],
            recv_sem=rx.at[turn, k], device_id={"pair": lax.rem(x + k + 1, NX) * NZ + z},
            device_id_type=MESH,
        )

    def deal(turn, q, h):
        return pltpu.make_async_remote_copy(
            src_ref=zsend.at[turn, q, h], dst_ref=zrecv.at[turn, z], send_sem=sz.at[turn, q, h],
            recv_sem=rz.at[turn, z],
            device_id={"pair": x * NZ + core * 8 + q, "ri": y * 2 + h}, device_id_type=MESH,
        )

    mine = lax.div(z, 8) == core
    zq = lax.rem(z, 8)

    def kept(turn):
        return pltpu.make_async_copy(zsend.at[turn, zq, core], zrecv.at[turn, z], local.at[3 + turn])

    def each(turn, do):
        for step in range(8):
            q = lax.rem(zq + step, 8)
            for h in range(2):
                if step == 0:

                    @pl.when(jnp.logical_not(mine & (core == h)))
                    def _():
                        do(deal(turn, q, h))
                else:
                    do(deal(turn, q, h))

    for turn in range(TURNS):

        @pl.when(lax.rem(z, TURNS) == turn)
        def _():
            own2.wait()

        def arrive(n, c):
            at = turn * SHARE + n

            @pl.when(at != slot(me))
            def _():
                pltpu.make_async_remote_copy(
                    src_ref=send2.at[0], dst_ref=recv2.at[at], send_sem=s2.at[0],
                    recv_sem=r2.at[at], device_id={"pair": me}, device_id_type=MESH,
                ).wait_recv()

            return c

        lax.fori_loop(0, SHARE, arrive, 0)
        for g in range(SHARE // 8):
            at = turn * SHARE + g * 8
            v = nn(pc[...], shifted(recv2[at : at + 8].reshape(192, 384), -1)).astype(BF)
            for mh in range(6):
                img[g * 32 : (g + 1) * 32, mh * 384 : (mh + 1) * 384] = v[mh * 32 : (mh + 1) * 32]
        for k in (1, 0, 2):
            xsend[turn, k] = part(lax.rem(x + k + 1, NX)).astype(BF)
            across(turn, k).start()
        total = part(x)
        for k in (1, 0, 2):
            across(turn, k).wait()
            total = total + xrecv[turn, k].astype(F32)
        total = total.astype(BF)
        for h in range(2):
            for q in range(8):
                zsend[turn, q, h] = total[q * ZROWS : (q + 1) * ZROWS, h * 256 : (h + 1) * 256]
        each(turn, lambda copy: copy.start())

        @pl.when(mine)
        def _():
            kept(turn).start()

    for turn in range(TURNS):
        each(turn, lambda copy: copy.wait_send())

        def dealt(fro):
            return pltpu.make_async_remote_copy(
                src_ref=zsend.at[0, 0, 0], dst_ref=zrecv.at[turn, fro], send_sem=sz.at[0, 0, 0],
                recv_sem=rz.at[turn, fro], device_id={"pair": me}, device_id_type=MESH,
            )

        @pl.when(mine)
        def _():
            kept(turn).wait()

        @pl.when(jnp.logical_not(mine))
        def _():
            dealt(z).wait_recv()

        def end3(k, c):
            dealt(lax.rem(z + k, NZ)).wait_recv()
            return c

        lax.fori_loop(1, NZ, end3, 0)
        some = zrecv[turn, 0].astype(F32)
        for k in range(1, NZ):
            some = some + zrecv[turn, k].astype(F32)
        for j in range(8 // TURNS):
            at = (j * TURNS + turn) * 4
            fsend[at : at + 4] = some[j * 4 : j * 4 + 4]

    @pl.when(x == y)
    def _():
        out[...] = fsend[...]

    @pl.when(x != y)
    def _():
        turn = pltpu.make_async_remote_copy(
            src_ref=fsend, dst_ref=out, send_sem=sf, recv_sem=rf,
            device_id={"pair": y * NZ + z, "ri": x * 2 + core}, device_id_type=MESH,
        )
        turn.start()
        turn.wait()

    def sent2(k, c):
        swap2(lax.rem(me + k, GROUPS)).wait_send()
        return c

    lax.fori_loop(1, GROUPS, sent2, 0)
    g_up.wait_send()
    g_down.wait_send()
    g_sib.wait_send()
    h_up.wait_send()
    h_down.wait_send()
    f_down.wait_send()
    f_up.wait_send()
    f_far.wait_send()


def on_device(tensor, pattern, pair_blocks, green_occ, green_virt):
    index = pair_blocks[:, 0] * NB + pair_blocks[:, 1]
    hits = index[None, :] == jnp.arange(NB * NB, dtype=jnp.int32)[:, None]
    order = jnp.arange(GROUPS, dtype=jnp.int32)[None, :]
    inverse = jnp.min(jnp.where(hits, order, GROUPS), axis=1).astype(jnp.int32)
    vmem = pl.BlockSpec(memory_space=pltpu.VMEM)
    smem = pl.BlockSpec(memory_space=pltpu.SMEM)
    dma = pltpu.SemaphoreType.DMA
    chi = pl.pallas_call(
        kernel,
        out_shape=jax.ShapeDtypeStruct((32, 256), F32),
        in_specs=[smem, smem, smem, vmem, vmem, vmem],
        out_specs=vmem,
        scratch_shapes=[
            pltpu.VMEM((GROUPS, 24, 384), BF),
            pltpu.VMEM((256, BB), BF),
            pltpu.VMEM((GROUPS + 1, 24, 384), BF),
            pltpu.VMEM((8, 256, BB), BF),
            pltpu.VMEM((4, 6, 2, 12, 32, 128), BF),
            pltpu.VMEM((4, 6, 2, 12, 32, 128), BF),
            pltpu.VMEM((GROUPS, 24, 384), BF),
            pltpu.VMEM((GROUPS, 24, 384), BF),
            pltpu.VMEM((SHARE * 4, BB), BF),
            pltpu.VMEM((TURNS, 3, SHARE * 4, 512), BF),
            pltpu.VMEM((TURNS, 3, SHARE * 4, 512), BF),
            pltpu.VMEM((TURNS, 8, 2, ZROWS, 256), BF),
            pltpu.VMEM((TURNS, NZ, ZROWS, 256), BF),
            pltpu.VMEM((32, 256), F32),
            pltpu.VMEM((768, 768), BF),
            pltpu.VMEM((768, 768), BF),
            pltpu.VMEM((192, 768), BF),
            dma((GROUPS,)), dma((GROUPS,)),
            dma((8,)), dma((8,)),
            dma((GROUPS,)), dma((GROUPS,)),
            dma((TURNS, 3)), dma((TURNS, 3)),
            dma((TURNS, 8, 2)), dma((TURNS, NZ)),
            dma, dma,
            dma((3 + TURNS,)),
        ],
        compiler_params=pltpu.CompilerParams(
            collective_id=0, has_side_effects=True, vmem_limit_bytes=60 << 20
        ),
    )(inverse, pair_blocks.T, pattern, tensor, green_virt, green_occ)
    return chi.T


def solution(mesh):
    in_specs = (P("pair", "ri", None), P("pair", "ri"), P(), P(), P())
    out_specs = P("ri", "pair")
    return jax.shard_map(
        on_device, mesh=mesh, in_specs=in_specs, out_specs=out_specs, check_vma=False
    )
```

```python
import jax
import jax.numpy as jnp
from jax import lax
from jax.experimental import pallas as pl
from jax.experimental.pallas import tpu as pltpu
from jax.sharding import PartitionSpec as P

BLK = 48
NB = 12
RB = 32
BB = 2304
NX, NY, NZ = 4, 4, 16
GROUPS = NX * NZ
TURNS = 2
SHARE = GROUPS // TURNS
ZT = NZ // TURNS
ZROWS = 32 // TURNS
MESH = pl.DeviceIdType.MESH
BF = jnp.bfloat16
F32 = jnp.float32


def nt(a, b):
    return lax.dot_general(a, b, (((1,), (1,)), ((), ())), preferred_element_type=F32)


def nn(a, b):
    return jnp.dot(a, b, preferred_element_type=F32)


def one_hot(rows, cols, match):
    r = lax.broadcasted_iota(jnp.int32, (rows, cols), 0)
    c = lax.broadcasted_iota(jnp.int32, (rows, cols), 1)
    return jnp.where(match(r, c), 1.0, 0.0).astype(BF)


def pad64(r, u):
    return (u == BLK * lax.div(r, 64) + lax.rem(r, 64)) & (lax.rem(r, 64) < BLK)


def pad32(r, u):
    b, w = lax.div(r, 384), lax.rem(r, 384)
    return (u == BLK * lax.div(w, 32) + 2 * lax.rem(w, 32) + b) & (lax.rem(w, 32) < 24)


def to_slab(r, c):
    d, w = lax.div(c, 192), lax.rem(c, 192)
    q = lax.rem(w, 4)
    at = lax.div(lax.rem(w, 32), 4) * 24 + lax.div(w, 32) * 4
    return r == at + lax.rem(q + 4 - d, 4)


def from_slab(r, c):
    d, w = lax.div(c, 192), lax.rem(c, 192)
    g, mh, rr = lax.div(w, 24), lax.div(lax.rem(w, 24), 4), lax.rem(w, 4)
    return r == mh * 32 + g * 4 + lax.rem(rr + d, 4)


def shifted(v, sign):
    row = lax.broadcasted_iota(jnp.int32, v.shape, 0)
    lane = lax.broadcasted_iota(jnp.int32, v.shape, 1)
    keep = lax.rem(row, 4) == lax.div(lane, 96)
    zero = jnp.zeros_like(v)
    rolled = [v] + [pltpu.roll(v, (sign * 96 * d) % 384, 1) for d in (1, 2, 3)]
    return jnp.concatenate([jnp.where(keep, u, zero) for u in rolled], axis=0)


def kernel(
    pb, pb_rows, pattern, tensor, gv, go, out,
    send1, dm, recv1, dall, dense, ws, send2, recv2, img, held, xsend, xrecv, zsend, zrecv, fsend,
    gvp, gop, pc, holder, inv,
    s1, r1, sy, ry, s2, r2, sx, rx, sz, rz, sf, rf, local,
):
    me = lax.axis_index("pair")
    ri = lax.axis_index("ri")
    x, z = lax.div(me, NZ), lax.rem(me, NZ)
    y, core = lax.div(ri, 2), lax.rem(ri, 2)
    sib = y * 2 + 1 - core
    up = lax.rem(y + 1, NY) * 2 + core
    down = lax.rem(y + NY - 1, NY) * 2 + core
    far = lax.rem(y + 2, NY) * 2 + core

    bar = pltpu.get_barrier_semaphore()

    def greet(pair, r):
        pl.semaphore_signal(bar, inc=1, device_id={"pair": pair, "ri": r}, device_id_type=MESH)

    def greet_pair(k, c):
        greet(lax.rem(me + k, GROUPS), ri)
        return c

    lax.fori_loop(1, GROUPS, greet_pair, 0)
    for k in range(NZ):
        greet(x * NZ + lax.rem(z + k, NZ), sib)
    greet(me, up)
    greet(me, down)

    @pl.when(x != y)
    def _():
        greet(y * NZ + z, x * 2 + core)

    pairs = lax.broadcasted_iota(jnp.int32, (GROUPS, GROUPS), 0)
    same = pairs == lax.broadcasted_iota(jnp.int32, (GROUPS, GROUPS), 1)
    index = pb_rows[0:1] * NB + pb_rows[1:2]
    index = jnp.sum(jnp.where(same, index, 0), axis=1, keepdims=True)
    hits = index == lax.broadcasted_iota(jnp.int32, (GROUPS, 256), 1)
    order = lax.broadcasted_iota(jnp.int32, (GROUPS, 256), 0)
    holder[...] = jnp.broadcast_to(jnp.min(jnp.where(hits, order, GROUPS), axis=0, keepdims=True), (8, 256))
    to_smem = pltpu.make_async_copy(holder, inv, local.at[3])
    to_smem.start()

    pc[...] = one_hot(192, 768, to_slab)

    def mask(g, c):
        rows = pl.ds(pl.multiple_of(g * RB, RB), RB)
        masked = tensor[0, rows] * pattern[0, g].astype(BF)
        dm[rows] = masked
        v = jnp.concatenate([masked[:, m * 384 : (m + 1) * 384] for m in range(6)], axis=0)
        send1[pl.ds(g * 8, 8)] = nn(pc[...], shifted(v, 1)).astype(BF).reshape(8, 24, 384)
        return c

    lax.fori_loop(0, 8, mask, 0)

    pl.semaphore_wait(bar, GROUPS - 1 + NZ + 2 + jnp.where(x != y, 1, 0))

    def along(src, dst, i, to):
        return pltpu.make_async_remote_copy(
            src_ref=src, dst_ref=dst, send_sem=sy.at[i], recv_sem=ry.at[i],
            device_id={"ri": to}, device_id_type=MESH,
        )

    def nth(n):
        turn, rest = lax.div(n, SHARE), lax.rem(n, SHARE)
        dx, dz = lax.div(rest, ZT), lax.rem(rest, ZT)
        return lax.rem(x + dx, NX) * NZ + lax.rem(lax.div(z, TURNS) + dz, ZT) * TURNS + turn

    def swap1(to):
        return pltpu.make_async_remote_copy(
            src_ref=send1.at[to], dst_ref=recv1.at[me], send_sem=s1.at[to], recv_sem=r1.at[me],
            device_id={"pair": to}, device_id_type=MESH,
        )

    def start1(n, c):
        to = nth(n)

        @pl.when(to != me)
        def _():
            swap1(to).start()

        return c

    g_up = along(dm, dall.at[ri], 0, up)
    g_down = along(dm, dall.at[ri], 1, down)
    g_sib = along(dm, dall.at[ri], 2, sib)
    lax.fori_loop(0, GROUPS, start1, 0)
    g_up.start()
    g_down.start()
    g_sib.start()
    own1 = pltpu.make_async_copy(send1.at[me], recv1.at[me], local.at[0])
    own1.start()
    ownd = pltpu.make_async_copy(dm, dall.at[ri], local.at[1])
    ownd.start()
    recv1[GROUPS] = jnp.zeros((24, 384), BF)

    e = one_hot(768, 576, pad64)
    gvp[...] = nt(nt(e, gv[...]).astype(BF), e).astype(BF)
    f = one_hot(768, 576, pad32)
    gop[...] = nt(nn(f, go[...]).astype(BF), f).astype(BF)
    pc[...] = one_hot(192, 768, from_slab)

    half = pl.ds(0, 128)
    rest = pl.ds(128, 128)
    along(dm, dall.at[down], 0, up).wait_recv()
    h_up = along(dall.at[down, half], dall.at[down, half], 3, up)
    h_up.start()
    f_down = along(dall.at[down], dall.at[down], 4, sib)
    f_down.start()
    along(dm, dall.at[up], 1, down).wait_recv()
    h_down = along(dall.at[up, rest], dall.at[up, rest], 5, down)
    h_down.start()
    f_up = along(dall.at[up], dall.at[up], 6, sib)
    f_up.start()

    own1.wait()
    to_smem.wait()

    def end1(k, c):
        fro = lax.rem(me + k, GROUPS)
        pltpu.make_async_remote_copy(
            src_ref=send1.at[fro], dst_ref=recv1.at[fro], send_sem=s1.at[fro],
            recv_sem=r1.at[fro], device_id={"pair": fro}, device_id_type=MESH,
        ).wait()
        return c

    lax.fori_loop(1, GROUPS, end1, 0)

    lane = lax.broadcasted_iota(jnp.int32, (32, 128), 1)

    def cut(tiles, n, at):
        t, low = n * BLK // 128, n * BLK % 128
        piece = pltpu.roll(tiles[t], (at - low) % 128, 1)
        if low + BLK > 128:
            more = pltpu.roll(tiles[t + 1], (at - low) % 128, 1)
            piece = jnp.where(lane < at + 128 - low, piece, more)
        return piece

    def place(n, c):
        i, jp = lax.div(n, 6), lax.rem(n, 6)
        low = jnp.zeros((8, 128), BF)

        def tiles(p):
            return [
                jnp.concatenate([recv1[p, :, t * 128 : (t + 1) * 128], low], axis=0)
                for t in range(3)
            ]

        b0, b1 = tiles(inv[0, 2 * n]), tiles(inv[0, 2 * n + 1])
        for a in range(8):
            dense[a // 2, jp, a % 2, i] = jnp.where(lane < 64, cut(b0, a, 0), cut(b1, a, 64))
        return c

    lax.fori_loop(0, 72, place, 0, unroll=4)

    def image(q, c):
        d = jnp.concatenate([dense[q, jp].reshape(768, 128) for jp in range(6)], axis=1)
        h = nn(d, gvp[...]).astype(BF)
        v = nn(gop[...], h).astype(BF)
        for tp in range(6):
            ws[q, tp] = v[:, tp * 128 : (tp + 1) * 128].reshape(2, 12, 32, 128)
        return c

    lax.fori_loop(0, 4, image, 0)

    def pack(p):
        l, t = pb[0, p], pb[1, p]
        tp, odd = lax.div(t, 2), lax.rem(t, 2)
        rolled = []
        for a in range(8):
            w = ws[a // 2, tp, a % 2, l]
            at = a * BLK % 128
            rolled.append(jnp.where(odd == 1, pltpu.roll(w, (at + 64) % 128, 1), pltpu.roll(w, at, 1)))
        for t in range(3):
            out_tile = None
            for a in reversed(range(8)):
                first, last = a * BLK - t * 128, (a + 1) * BLK - t * 128
                if last > 0 and first < 128:
                    if out_tile is None:
                        out_tile = rolled[a]
                    else:
                        out_tile = jnp.where(lane < last, rolled[a], out_tile)
            send2[p, :, t * 128 : (t + 1) * 128] = out_tile[:24]

    def slot(pair):
        w = lax.rem(pair, NZ)
        return lax.rem(w, TURNS) * SHARE + lax.div(pair, NZ) * ZT + lax.div(w, TURNS)

    def swap2(to):
        return pltpu.make_async_remote_copy(
            src_ref=send2.at[to], dst_ref=recv2.at[slot(me)], send_sem=s2.at[to],
            recv_sem=r2.at[slot(me)], device_id={"pair": to}, device_id_type=MESH,
        )

    def start2(k, c):
        to = lax.rem(me + k, GROUPS)
        pack(to)
        swap2(to).start()
        return c

    lax.fori_loop(1, GROUPS, start2, 0, unroll=3)
    pack(me)
    own2 = pltpu.make_async_copy(send2.at[me], recv2.at[slot(me)], local.at[2])
    own2.start()

    along(dm.at[half], dall.at[far, half], 3, up).wait_recv()
    along(dm.at[rest], dall.at[far, rest], 5, down).wait_recv()
    f_far = along(dall.at[far], dall.at[far], 7, sib)
    f_far.start()
    ownd.wait()
    g_sib.wait_recv()
    f_down.wait_recv()
    f_up.wait_recv()
    f_far.wait_recv()

    def across(turn, k, h):
        return pltpu.make_async_remote_copy(
            src_ref=xsend.at[turn, k, h], dst_ref=xrecv.at[turn, k, h],
            send_sem=sx.at[turn, k, h], recv_sem=rx.at[turn, k, h],
            device_id={"pair": lax.rem(x + k + 1, NX) * NZ + z}, device_id_type=MESH,
        )

    def deal(turn, q, h):
        return pltpu.make_async_remote_copy(
            src_ref=zsend.at[turn, q, h], dst_ref=zrecv.at[turn, z], send_sem=sz.at[turn, q, h],
            recv_sem=rz.at[turn, z],
            device_id={"pair": x * NZ + core * 8 + q, "ri": y * 2 + h}, device_id_type=MESH,
        )

    mine = lax.div(z, 8) == core
    zq = lax.rem(z, 8)

    def kept(turn):
        return pltpu.make_async_copy(zsend.at[turn, zq, core], zrecv.at[turn, z], local.at[3 + turn])

    def each(turn, h, do):
        def one(step, c):
            @pl.when(jnp.logical_not((step == 0) & mine & (core == h)))
            def _():
                do(deal(turn, lax.rem(zq + step, 8), h))

            return c

        lax.fori_loop(0, 8, one, 0)

    g_up.wait_send()
    g_down.wait_send()
    g_sib.wait_send()
    h_up.wait_send()
    h_down.wait_send()
    f_down.wait_send()
    f_up.wait_send()

    def sent2(k, c):
        swap2(lax.rem(me + k, GROUPS)).wait_send()
        return c

    def add_up(turn, c):
        @pl.when(turn == TURNS - 1)
        def _():
            lax.fori_loop(1, GROUPS, sent2, 0)
            f_far.wait_send()

        @pl.when(lax.rem(z, TURNS) == turn)
        def _():
            own2.wait()

        def arrive(n, c):
            at = turn * SHARE + n

            @pl.when(at != slot(me))
            def _():
                pltpu.make_async_remote_copy(
                    src_ref=send2.at[0], dst_ref=recv2.at[at], send_sem=s2.at[0],
                    recv_sem=r2.at[at], device_id={"pair": me}, device_id_type=MESH,
                ).wait_recv()

            return c

        lax.fori_loop(0, SHARE, arrive, 0)
        def gather(g, c):
            v = shifted(recv2[pl.ds(turn * SHARE + g * 8, 8)].reshape(192, 384), -1)
            v = nn(pc[...], v).astype(BF)
            rows = pl.ds(pl.multiple_of(g * 32, 32), 32)
            for mh in range(6):
                img[rows, mh * 384 : (mh + 1) * 384] = v[mh * 32 : (mh + 1) * 32]
            return c

        lax.fori_loop(0, SHARE // 8, gather, 0)

        def part(n, c):
            step, h = lax.div(n, 2), lax.rem(n, 2)
            far_x = lax.rem(lax.rem(step + 1, 3) + 1, 4)
            to_x = jnp.where(step == 3, 0, far_x)
            held[h] = nt(img[...], dall[2 * lax.rem(x + to_x, NX) + h])

            @pl.when(step < 3)
            def _():
                k = lax.rem(step + 1, 3)
                xsend[turn, k, h] = held[h].astype(BF)
                across(turn, k, h).start()

            return c

        lax.fori_loop(0, 8, part, 0)

        def onward(h, c):
            total = held[h]
            for k in range(3):
                across(turn, k, h).wait()
                total = total + xrecv[turn, k, h].astype(F32)
            total = total.astype(BF)
            for q in range(8):
                zsend[turn, q, h] = total[q * ZROWS : (q + 1) * ZROWS]
            each(turn, h, lambda copy: copy.start())

            @pl.when(mine & (core == h))
            def _():
                kept(turn).start()

            return c

        lax.fori_loop(0, 2, onward, 0)
        return c

    lax.fori_loop(0, TURNS, add_up, 0)

    for turn in range(TURNS):

        def dealt(fro):
            return pltpu.make_async_remote_copy(
                src_ref=zsend.at[0, 0, 0], dst_ref=zrecv.at[turn, fro], send_sem=sz.at[0, 0, 0],
                recv_sem=rz.at[turn, fro], device_id={"pair": me}, device_id_type=MESH,
            )

        @pl.when(mine)
        def _():
            kept(turn).wait()

        @pl.when(jnp.logical_not(mine))
        def _():
            dealt(z).wait_recv()

        def end3(k, c):
            dealt(lax.rem(z + k, NZ)).wait_recv()
            return c

        lax.fori_loop(1, NZ, end3, 0)
        some = zrecv[turn, 0].astype(F32)
        for k in range(1, NZ):
            some = some + zrecv[turn, k].astype(F32)
        for j in range(8 // TURNS):
            at = (j * TURNS + turn) * 4
            fsend[at : at + 4] = some[j * 4 : j * 4 + 4]

    @pl.when(x == y)
    def _():
        out[...] = fsend[...]

    turned = pltpu.make_async_remote_copy(
        src_ref=fsend, dst_ref=out, send_sem=sf, recv_sem=rf,
        device_id={"pair": y * NZ + z, "ri": x * 2 + core}, device_id_type=MESH,
    )

    @pl.when(x != y)
    def _():
        turned.start()

    for turn in range(TURNS):
        for h in range(2):
            each(turn, h, lambda copy: copy.wait_send())

    @pl.when(x != y)
    def _():
        turned.wait()


def on_device(tensor, pattern, pair_blocks, green_occ, green_virt):
    vmem = pl.BlockSpec(memory_space=pltpu.VMEM)
    smem = pl.BlockSpec(memory_space=pltpu.SMEM)
    dma = pltpu.SemaphoreType.DMA
    chi = pl.pallas_call(
        kernel,
        out_shape=jax.ShapeDtypeStruct((32, 256), F32),
        in_specs=[smem, vmem, smem, vmem, vmem, vmem],
        out_specs=vmem,
        scratch_shapes=[
            pltpu.VMEM((GROUPS, 24, 384), BF),
            pltpu.VMEM((256, BB), BF),
            pltpu.VMEM((GROUPS + 1, 24, 384), BF),
            pltpu.VMEM((8, 256, BB), BF),
            pltpu.VMEM((4, 6, 2, 12, 32, 128), BF),
            pltpu.VMEM((4, 6, 2, 12, 32, 128), BF),
            pltpu.VMEM((GROUPS, 24, 384), BF),
            pltpu.VMEM((GROUPS, 24, 384), BF),
            pltpu.VMEM((SHARE * 4, BB), BF),
            pltpu.VMEM((2, SHARE * 4, 256), F32),
            pltpu.VMEM((TURNS, 3, 2, SHARE * 4, 256), BF),
            pltpu.VMEM((TURNS, 3, 2, SHARE * 4, 256), BF),
            pltpu.VMEM((TURNS, 8, 2, ZROWS, 256), BF),
            pltpu.VMEM((TURNS, NZ, ZROWS, 256), BF),
            pltpu.VMEM((32, 256), F32),
            pltpu.VMEM((768, 768), BF),
            pltpu.VMEM((768, 768), BF),
            pltpu.VMEM((192, 768), BF),
            pltpu.VMEM((8, 256), jnp.int32),
            pltpu.SMEM((8, 256), jnp.int32),
            dma((GROUPS,)), dma((GROUPS,)),
            dma((8,)), dma((8,)),
            dma((GROUPS,)), dma((GROUPS,)),
            dma((TURNS, 3, 2)), dma((TURNS, 3, 2)),
            dma((TURNS, 8, 2)), dma((TURNS, NZ)),
            dma, dma,
            dma((3 + TURNS,)),
        ],
        compiler_params=pltpu.CompilerParams(
            collective_id=0, has_side_effects=True, vmem_limit_bytes=60 << 20
        ),
    )(pair_blocks.T, pair_blocks.T, pattern, tensor, green_virt, green_occ)
    return chi.T


def solution(mesh):
    in_specs = (P("pair", "ri", None), P("pair", "ri"), P(), P(), P())
    out_specs = P("ri", "pair")
    return jax.shard_map(
        on_device, mesh=mesh, in_specs=in_specs, out_specs=out_specs, check_vma=False
    )
```

```python
import jax
import jax.numpy as jnp
from jax import lax
from jax.experimental import pallas as pl
from jax.experimental.pallas import tpu as pltpu
from jax.sharding import PartitionSpec as P

BLK = 48
NB = 12
RB = 32
BB = 2304
NX, NY, NZ = 4, 4, 16
GROUPS = NX * NZ
TURNS = 2
SHARE = GROUPS // TURNS
ZT = NZ // TURNS
ZROWS = 32 // TURNS
MESH = pl.DeviceIdType.MESH
BF = jnp.bfloat16
F32 = jnp.float32


def nt(a, b):
    return lax.dot_general(a, b, (((1,), (1,)), ((), ())), preferred_element_type=F32)


def nn(a, b):
    return jnp.dot(a, b, preferred_element_type=F32)


def one_hot(rows, cols, match):
    r = lax.broadcasted_iota(jnp.int32, (rows, cols), 0)
    c = lax.broadcasted_iota(jnp.int32, (rows, cols), 1)
    return jnp.where(match(r, c), 1.0, 0.0).astype(BF)


def pad64(r, u):
    return (u == BLK * lax.div(r, 64) + lax.rem(r, 64)) & (lax.rem(r, 64) < BLK)


def pad32(r, u):
    b, w = lax.div(r, 384), lax.rem(r, 384)
    return (u == BLK * lax.div(w, 32) + 2 * lax.rem(w, 32) + b) & (lax.rem(w, 32) < 24)


def to_slab(r, c):
    d, w = lax.div(c, 192), lax.rem(c, 192)
    q = lax.rem(w, 4)
    at = lax.div(lax.rem(w, 32), 4) * 24 + lax.div(w, 32) * 4
    return r == at + lax.rem(q + 4 - d, 4)


def from_slab(r, c):
    d, w = lax.div(c, 192), lax.rem(c, 192)
    g, mh, rr = lax.div(w, 24), lax.div(lax.rem(w, 24), 4), lax.rem(w, 4)
    return r == mh * 32 + g * 4 + lax.rem(rr + d, 4)


def shifted(v, sign):
    row = lax.broadcasted_iota(jnp.int32, v.shape, 0)
    lane = lax.broadcasted_iota(jnp.int32, v.shape, 1)
    keep = lax.rem(row, 4) == lax.div(lane, 96)
    zero = jnp.zeros_like(v)
    rolled = [v] + [pltpu.roll(v, (sign * 96 * d) % 384, 1) for d in (1, 2, 3)]
    return jnp.concatenate([jnp.where(keep, u, zero) for u in rolled], axis=0)


def kernel(
    pb, pb_rows, pattern, tensor, gv, go, out,
    send1, dm, recv1, dall, dense, ws, send2, recv2, img, held, xsend, xrecv, zsend, zrecv, fsend,
    gvp, gop, pc, holder, inv,
    s1, r1, sy, ry, s2, r2, sx, rx, sz, rz, sf, rf, local,
):
    me = lax.axis_index("pair")
    ri = lax.axis_index("ri")
    x, z = lax.div(me, NZ), lax.rem(me, NZ)
    y, core = lax.div(ri, 2), lax.rem(ri, 2)
    sib = y * 2 + 1 - core
    up = lax.rem(y + 1, NY) * 2 + core
    down = lax.rem(y + NY - 1, NY) * 2 + core
    far = lax.rem(y + 2, NY) * 2 + core

    bar = pltpu.get_barrier_semaphore()

    def greet(pair, r):
        pl.semaphore_signal(bar, inc=1, device_id={"pair": pair, "ri": r}, device_id_type=MESH)

    def greet_pair(k, c):
        greet(lax.rem(me + k, GROUPS), ri)
        return c

    lax.fori_loop(1, GROUPS, greet_pair, 0)
    for k in range(NZ):
        greet(x * NZ + lax.rem(z + k, NZ), sib)
    greet(me, up)
    greet(me, down)

    @pl.when(x != y)
    def _():
        greet(y * NZ + z, x * 2 + core)

    pairs = lax.broadcasted_iota(jnp.int32, (GROUPS, GROUPS), 0)
    same = pairs == lax.broadcasted_iota(jnp.int32, (GROUPS, GROUPS), 1)
    index = pb_rows[0:1] * NB + pb_rows[1:2]
    index = jnp.sum(jnp.where(same, index, 0), axis=1, keepdims=True)
    hits = index == lax.broadcasted_iota(jnp.int32, (GROUPS, 256), 1)
    order = lax.broadcasted_iota(jnp.int32, (GROUPS, 256), 0)
    holder[...] = jnp.broadcast_to(jnp.min(jnp.where(hits, order, GROUPS), axis=0, keepdims=True), (8, 256))
    to_smem = pltpu.make_async_copy(holder, inv, local.at[3])
    to_smem.start()

    pc[...] = one_hot(192, 768, to_slab)

    def mask(g, c):
        rows = pl.ds(pl.multiple_of(g * RB, RB), RB)
        masked = tensor[0, rows] * pattern[0, g].astype(BF)
        dm[rows] = masked
        v = jnp.concatenate([masked[:, m * 384 : (m + 1) * 384] for m in range(6)], axis=0)
        send1[pl.ds(g * 8, 8)] = nn(pc[...], shifted(v, 1)).astype(BF).reshape(8, 24, 384)
        return c

    lax.fori_loop(0, 8, mask, 0)

    pl.semaphore_wait(bar, GROUPS - 1 + NZ + 2 + jnp.where(x != y, 1, 0))

    def along(src, dst, i, to):
        return pltpu.make_async_remote_copy(
            src_ref=src, dst_ref=dst, send_sem=sy.at[i], recv_sem=ry.at[i],
            device_id={"ri": to}, device_id_type=MESH,
        )

    def nth(n):
        turn, rest = lax.div(n, SHARE), lax.rem(n, SHARE)
        dx, dz = lax.div(rest, ZT), lax.rem(rest, ZT)
        return lax.rem(x + dx, NX) * NZ + lax.rem(lax.div(z, TURNS) + dz, ZT) * TURNS + turn

    def swap1(to):
        return pltpu.make_async_remote_copy(
            src_ref=send1.at[to], dst_ref=recv1.at[me], send_sem=s1.at[to], recv_sem=r1.at[me],
            device_id={"pair": to}, device_id_type=MESH,
        )

    def start1(n, c):
        to = nth(n)

        @pl.when(to != me)
        def _():
            swap1(to).start()

        return c

    g_up = along(dm, dall.at[ri], 0, up)
    g_down = along(dm, dall.at[ri], 1, down)
    g_sib = along(dm, dall.at[ri], 2, sib)
    lax.fori_loop(0, GROUPS, start1, 0)
    g_up.start()
    g_down.start()
    g_sib.start()
    own1 = pltpu.make_async_copy(send1.at[me], recv1.at[me], local.at[0])
    own1.start()
    ownd = pltpu.make_async_copy(dm, dall.at[ri], local.at[1])
    ownd.start()
    recv1[GROUPS] = jnp.zeros((24, 384), BF)

    e = one_hot(768, 576, pad64)
    gvp[...] = nt(nt(e, gv[...]).astype(BF), e).astype(BF)
    f = one_hot(768, 576, pad32)
    gop[...] = nt(nn(f, go[...]).astype(BF), f).astype(BF)
    pc[...] = one_hot(192, 768, from_slab)

    half = pl.ds(0, 128)
    rest = pl.ds(128, 128)
    along(dm, dall.at[down], 0, up).wait_recv()
    h_up = along(dall.at[down, half], dall.at[down, half], 3, up)
    h_up.start()
    f_down = along(dall.at[down], dall.at[down], 4, sib)
    f_down.start()
    along(dm, dall.at[up], 1, down).wait_recv()
    h_down = along(dall.at[up, rest], dall.at[up, rest], 5, down)
    h_down.start()
    f_up = along(dall.at[up], dall.at[up], 6, sib)
    f_up.start()

    own1.wait()
    to_smem.wait()

    def end1(k, c):
        fro = lax.rem(me + k, GROUPS)
        pltpu.make_async_remote_copy(
            src_ref=send1.at[fro], dst_ref=recv1.at[fro], send_sem=s1.at[fro],
            recv_sem=r1.at[fro], device_id={"pair": fro}, device_id_type=MESH,
        ).wait()
        return c

    lax.fori_loop(1, GROUPS, end1, 0)

    lane = lax.broadcasted_iota(jnp.int32, (32, 128), 1)

    def cut(tiles, n, at):
        t, low = n * BLK // 128, n * BLK % 128
        piece = pltpu.roll(tiles[t], (at - low) % 128, 1)
        if low + BLK > 128:
            more = pltpu.roll(tiles[t + 1], (at - low) % 128, 1)
            piece = jnp.where(lane < at + 128 - low, piece, more)
        return piece

    def place(n, c):
        i, jp = lax.div(n, 6), lax.rem(n, 6)
        low = jnp.zeros((8, 128), BF)

        def tiles(p):
            return [
                jnp.concatenate([recv1[p, :, t * 128 : (t + 1) * 128], low], axis=0)
                for t in range(3)
            ]

        b0, b1 = tiles(inv[0, 2 * n]), tiles(inv[0, 2 * n + 1])
        for a in range(8):
            dense[a // 2, jp, a % 2, i] = jnp.where(lane < 64, cut(b0, a, 0), cut(b1, a, 64))
        return c

    lax.fori_loop(0, 72, place, 0, unroll=8)

    def image(q, c):
        d = jnp.concatenate([dense[q, jp].reshape(768, 128) for jp in range(6)], axis=1)
        h = nn(d, gvp[...]).astype(BF)
        v = nn(gop[...], h).astype(BF)
        for tp in range(6):
            ws[q, tp] = v[:, tp * 128 : (tp + 1) * 128].reshape(2, 12, 32, 128)
        return c

    lax.fori_loop(0, 4, image, 0)

    def pack(p):
        l, t = pb[0, p], pb[1, p]
        tp, odd = lax.div(t, 2), lax.rem(t, 2)
        rolled = []
        for a in range(8):
            w = ws[a // 2, tp, a % 2, l]
            at = a * BLK % 128
            rolled.append(jnp.where(odd == 1, pltpu.roll(w, (at + 64) % 128, 1), pltpu.roll(w, at, 1)))
        for t in range(3):
            out_tile = None
            for a in reversed(range(8)):
                first, last = a * BLK - t * 128, (a + 1) * BLK - t * 128
                if last > 0 and first < 128:
                    if out_tile is None:
                        out_tile = rolled[a]
                    else:
                        out_tile = jnp.where(lane < last, rolled[a], out_tile)
            send2[p, :, t * 128 : (t + 1) * 128] = out_tile[:24]

    def slot(pair):
        w = lax.rem(pair, NZ)
        return lax.rem(w, TURNS) * SHARE + lax.div(pair, NZ) * ZT + lax.div(w, TURNS)

    def swap2(to):
        return pltpu.make_async_remote_copy(
            src_ref=send2.at[to], dst_ref=recv2.at[slot(me)], send_sem=s2.at[to],
            recv_sem=r2.at[slot(me)], device_id={"pair": to}, device_id_type=MESH,
        )

    def start2(k, c):
        to = lax.rem(me + k, GROUPS)
        pack(to)
        swap2(to).start()
        return c

    lax.fori_loop(1, GROUPS, start2, 0, unroll=7)
    pack(me)
    own2 = pltpu.make_async_copy(send2.at[me], recv2.at[slot(me)], local.at[2])
    own2.start()

    along(dm.at[half], dall.at[far, half], 3, up).wait_recv()
    along(dm.at[rest], dall.at[far, rest], 5, down).wait_recv()
    f_far = along(dall.at[far], dall.at[far], 7, sib)
    f_far.start()
    ownd.wait()
    g_sib.wait_recv()
    f_down.wait_recv()
    f_up.wait_recv()
    f_far.wait_recv()

    def across(turn, k, h):
        return pltpu.make_async_remote_copy(
            src_ref=xsend.at[turn, k, h], dst_ref=xrecv.at[turn, k, h],
            send_sem=sx.at[turn, k, h], recv_sem=rx.at[turn, k, h],
            device_id={"pair": lax.rem(x + k + 1, NX) * NZ + z}, device_id_type=MESH,
        )

    def deal(turn, q, h):
        return pltpu.make_async_remote_copy(
            src_ref=zsend.at[turn, q, h], dst_ref=zrecv.at[turn, z], send_sem=sz.at[turn, q, h],
            recv_sem=rz.at[turn, z],
            device_id={"pair": x * NZ + core * 8 + q, "ri": y * 2 + h}, device_id_type=MESH,
        )

    mine = lax.div(z, 8) == core
    zq = lax.rem(z, 8)

    def kept(turn):
        return pltpu.make_async_copy(zsend.at[turn, zq, core], zrecv.at[turn, z], local.at[3 + turn])

    def each(turn, h, do):
        def one(step, c):
            @pl.when(jnp.logical_not((step == 0) & mine & (core == h)))
            def _():
                do(deal(turn, lax.rem(zq + step, 8), h))

            return c

        lax.fori_loop(0, 8, one, 0)

    g_up.wait_send()
    g_down.wait_send()
    g_sib.wait_send()
    h_up.wait_send()
    h_down.wait_send()
    f_down.wait_send()
    f_up.wait_send()

    def sent2(k, c):
        swap2(lax.rem(me + k, GROUPS)).wait_send()
        return c

    def add_up(turn, c):
        @pl.when(turn == TURNS - 1)
        def _():
            lax.fori_loop(1, GROUPS, sent2, 0)
            f_far.wait_send()

        @pl.when(lax.rem(z, TURNS) == turn)
        def _():
            own2.wait()

        def arrive(n, c):
            at = turn * SHARE + n

            @pl.when(at != slot(me))
            def _():
                pltpu.make_async_remote_copy(
                    src_ref=send2.at[0], dst_ref=recv2.at[at], send_sem=s2.at[0],
                    recv_sem=r2.at[at], device_id={"pair": me}, device_id_type=MESH,
                ).wait_recv()

            return c

        lax.fori_loop(0, SHARE, arrive, 0)
        def gather(g, c):
            v = shifted(recv2[pl.ds(turn * SHARE + g * 8, 8)].reshape(192, 384), -1)
            v = nn(pc[...], v).astype(BF)
            rows = pl.ds(pl.multiple_of(g * 32, 32), 32)
            for mh in range(6):
                img[rows, mh * 384 : (mh + 1) * 384] = v[mh * 32 : (mh + 1) * 32]
            return c

        lax.fori_loop(0, SHARE // 8, gather, 0)

        def part(n, c):
            step, h = lax.rem(n, 4), lax.div(n, 4)
            far_x = lax.rem(lax.rem(step + 1, 3) + 1, 4)
            to_x = jnp.where(step == 3, 0, far_x)
            held[h] = nt(img[...], dall[2 * lax.rem(x + to_x, NX) + h])

            @pl.when(step < 3)
            def _():
                k = lax.rem(step + 1, 3)
                xsend[turn, k, h] = held[h].astype(BF)
                across(turn, k, h).start()

            return c

        lax.fori_loop(0, 8, part, 0)

        def onward(h, c):
            total = held[h]
            for k in range(3):
                across(turn, k, h).wait()
                total = total + xrecv[turn, k, h].astype(F32)
            total = total.astype(BF)
            for q in range(8):
                zsend[turn, q, h] = total[q * ZROWS : (q + 1) * ZROWS]
            each(turn, h, lambda copy: copy.start())

            @pl.when(mine & (core == h))
            def _():
                kept(turn).start()

            return c

        lax.fori_loop(0, 2, onward, 0)
        return c

    lax.fori_loop(0, TURNS, add_up, 0)

    for turn in range(TURNS):

        def dealt(fro):
            return pltpu.make_async_remote_copy(
                src_ref=zsend.at[0, 0, 0], dst_ref=zrecv.at[turn, fro], send_sem=sz.at[0, 0, 0],
                recv_sem=rz.at[turn, fro], device_id={"pair": me}, device_id_type=MESH,
            )

        @pl.when(mine)
        def _():
            kept(turn).wait()

        @pl.when(jnp.logical_not(mine))
        def _():
            dealt(z).wait_recv()

        def end3(k, c):
            dealt(lax.rem(z + k, NZ)).wait_recv()
            return c

        lax.fori_loop(1, NZ, end3, 0)
        some = zrecv[turn, 0].astype(F32)
        for k in range(1, NZ):
            some = some + zrecv[turn, k].astype(F32)
        for j in range(8 // TURNS):
            at = (j * TURNS + turn) * 4
            fsend[at : at + 4] = some[j * 4 : j * 4 + 4]

    @pl.when(x == y)
    def _():
        out[...] = fsend[...]

    turned = pltpu.make_async_remote_copy(
        src_ref=fsend, dst_ref=out, send_sem=sf, recv_sem=rf,
        device_id={"pair": y * NZ + z, "ri": x * 2 + core}, device_id_type=MESH,
    )

    @pl.when(x != y)
    def _():
        turned.start()

    for turn in range(TURNS):
        for h in range(2):
            each(turn, h, lambda copy: copy.wait_send())

    @pl.when(x != y)
    def _():
        turned.wait()


def on_device(tensor, pattern, pair_blocks, green_occ, green_virt):
    vmem = pl.BlockSpec(memory_space=pltpu.VMEM)
    smem = pl.BlockSpec(memory_space=pltpu.SMEM)
    dma = pltpu.SemaphoreType.DMA
    chi = pl.pallas_call(
        kernel,
        out_shape=jax.ShapeDtypeStruct((32, 256), F32),
        in_specs=[smem, vmem, smem, vmem, vmem, vmem],
        out_specs=vmem,
        scratch_shapes=[
            pltpu.VMEM((GROUPS, 24, 384), BF),
            pltpu.VMEM((256, BB), BF),
            pltpu.VMEM((GROUPS + 1, 24, 384), BF),
            pltpu.VMEM((8, 256, BB), BF),
            pltpu.VMEM((4, 6, 2, 12, 32, 128), BF),
            pltpu.VMEM((4, 6, 2, 12, 32, 128), BF),
            pltpu.VMEM((GROUPS, 24, 384), BF),
            pltpu.VMEM((GROUPS, 24, 384), BF),
            pltpu.VMEM((SHARE * 4, BB), BF),
            pltpu.VMEM((2, SHARE * 4, 256), F32),
            pltpu.VMEM((TURNS, 3, 2, SHARE * 4, 256), BF),
            pltpu.VMEM((TURNS, 3, 2, SHARE * 4, 256), BF),
            pltpu.VMEM((TURNS, 8, 2, ZROWS, 256), BF),
            pltpu.VMEM((TURNS, NZ, ZROWS, 256), BF),
            pltpu.VMEM((32, 256), F32),
            pltpu.VMEM((768, 768), BF),
            pltpu.VMEM((768, 768), BF),
            pltpu.VMEM((192, 768), BF),
            pltpu.VMEM((8, 256), jnp.int32),
            pltpu.SMEM((8, 256), jnp.int32),
            dma((GROUPS,)), dma((GROUPS,)),
            dma((8,)), dma((8,)),
            dma((GROUPS,)), dma((GROUPS,)),
            dma((TURNS, 3, 2)), dma((TURNS, 3, 2)),
            dma((TURNS, 8, 2)), dma((TURNS, NZ)),
            dma, dma,
            dma((3 + TURNS,)),
        ],
        compiler_params=pltpu.CompilerParams(
            collective_id=0, has_side_effects=True, vmem_limit_bytes=60 << 20
        ),
    )(pair_blocks.T, pair_blocks.T, pattern, tensor, green_virt, green_occ)
    return chi.T


def solution(mesh):
    in_specs = (P("pair", "ri", None), P("pair", "ri"), P(), P(), P())
    out_specs = P("ri", "pair")
    return jax.shard_map(
        on_device, mesh=mesh, in_specs=in_specs, out_specs=out_specs, check_vma=False
    )
```
